768 devices in a mesh: inter: 16 (over x, z_lo), intra: 48 (over z_hi, y, core).
Axes of the slice: x: 4, y: 8, z: 12 (z_hi: 3, z_lo: 4; z = z_hi * 4 + z_lo), core: 2. Of those that a mesh axis runs over, the one named last changes fastest.
Arguments:
- layer_input: bfloat16 [98304, 4608], P(('inter', 'intra')), may hold values from -80 to 80
- norm_gain: bfloat16 [4608], P('intra'), may hold values from 0.5 to 1.5
- kv_weight: bfloat16 [4608, 128], P('intra'), may hold values from -0.09375 to 0.09375
- kv_cotangent: bfloat16 [98304, 128], P(('inter', 'intra')), may hold values from -24 to 24
Outputs:
- input_grad: bfloat16 [98304, 4608], P(('inter', 'intra'))
- weight_grad: float32 [4608, 128], P(('inter', 'intra'))
- gain_grad: float32 [4608], P(('inter', 'intra'))
The draws below stay inside these ranges and needn't reach their ends.
All inputs are finite; a program needn't handle non-finite values.
Results may differ from the reference program's by a relative error of at most 0.0029.
Values may be sent and summed in bfloat16 or wider, within the bound.
No kernel may reach another device: no remote copies, remote signals or barrier semaphores. Data moves between devices by JAX's collectives and lax.ppermute only.
A program may use at most 64 MiB of HBM per device.

```python
import math
import jax
import jax.numpy as jnp
from jax import lax

D = 4608
HD = 64
TOK_DEV = 128
TOKENS = 98304
N_INTER = 16
N_INTRA = 48


def draw_layer_input(key, part):
    key_base = jax.random.fold_in(key, 11)
    key_rows = jax.random.fold_in(key, 12)
    key_cols = jax.random.fold_in(key, 13)
    values = jnp.clip(jax.random.normal(key_base, (TOKENS, D), jnp.float32), -4.0, 4.0)
    lowest = 0.3
    highest = 3.0
    row_scale = jnp.exp(jax.random.uniform(key_rows, (TOKENS, 1), jnp.float32, math.log(lowest), math.log(highest)))
    col_scale = jnp.exp(jax.random.uniform(key_cols, (1, D), jnp.float32, math.log(lowest), math.log(highest)))
    return (values * row_scale * col_scale).astype(jnp.bfloat16)


def block_levels(rng, dims, cuts, least, high):
    def one(position, parts):
        draws = jax.random.uniform(jax.random.fold_in(jax.random.fold_in(rng, 6), position), (parts,), jnp.float32, least / len(cuts), high / len(cuts))
        return jnp.repeat(jnp.exp(draws), dims[position] // parts).reshape((-1,) + (1,) * (len(dims) - position - 1))

    factor_of = one(*cuts[0])
    for cut in cuts[1:]:
        factor_of = factor_of * one(*cut)
    return factor_of


def centred(key, dims, spread, bound, cuts=(), kind=jnp.bfloat16):
    loudness = block_levels(key, dims, cuts, -0.22, 0.18) if cuts else 1.0
    values = jax.random.normal(key, dims, jnp.float32) * spread * loudness
    return jnp.minimum(jnp.maximum(values, -bound), bound).astype(kind)


def setup_inputs(seed: int = 0) -> dict:
    key_list = jax.random.split(jax.random.key(seed), 5)
    layer_input = draw_layer_input(jax.random.fold_in(key_list[4], 71), 0)
    norm_gain = jnp.clip(1.0 + 0.1 * jax.random.normal(key_list[1], (D,), jnp.float32), 0.5, 1.5).astype(jnp.bfloat16)
    kv_weight = centred(key_list[2], (D, 2 * HD), D ** -0.5, 0.09375, ((0, 48),))
    kv_cotangent = centred(key_list[3], (TOKENS, 2 * HD), 4.0, 24.0, ((0, 768),))
    return dict(layer_input=layer_input, norm_gain=norm_gain, kv_weight=kv_weight, kv_cotangent=kv_cotangent)


EPS = 1e-05

def reference(layer_input, norm_gain, kv_weight, kv_cotangent):
    devices = N_INTER * N_INTRA
    gain_wide = norm_gain.astype(jnp.float32)

    def block_step(carry, pieces):
        weight_sum, gain_sum = carry
        rows_in, cotangent = pieces
        widened = rows_in.astype(jnp.float32)
        inverse_rms = lax.rsqrt(lax.optimization_barrier(jnp.mean(widened * widened, axis=1, keepdims=True)) + EPS)
        normal_rows = widened * inverse_rms
        normed = (normal_rows * gain_wide).astype(jnp.bfloat16)
        weight_sum = weight_sum + jnp.dot(normed.T, cotangent, preferred_element_type=jnp.float32)
        feature_grad = jnp.dot(cotangent, kv_weight.T, preferred_element_type=jnp.float32)
        gain_sum = gain_sum + lax.optimization_barrier(jnp.sum(feature_grad * normal_rows, axis=0))
        scaled_grad = feature_grad * gain_wide
        centre = lax.optimization_barrier(jnp.mean(scaled_grad * normal_rows, axis=1, keepdims=True))
        result = (inverse_rms * (scaled_grad - normal_rows * centre)).astype(jnp.bfloat16)
        return ((weight_sum, gain_sum), result)
    blocks_in = layer_input.reshape(devices, TOK_DEV, D)
    blocks_cot = kv_cotangent.reshape(devices, TOK_DEV, 2 * HD)
    start = (jnp.zeros((D, 2 * HD), jnp.float32), jnp.zeros((D,), jnp.float32))
    (weight_sum, gain_sum), grads = lax.scan(block_step, start, (blocks_in, blocks_cot))
    input_grad = grads.reshape(TOKENS, D)
    return (input_grad, weight_sum / float(devices), gain_sum / float(devices))
```

```python
import jax
import jax.numpy as jnp
from jax import lax
from jax.experimental import pallas as pl
from jax.experimental.pallas import tpu as pltpu
from jax.sharding import Mesh, PartitionSpec as P

EPS = 1e-05
X, ZL, ZH, Y, C = 4, 4, 3, 8, 2
INTER, PEERS = X * ZL, ZH * Y
DEVICES = INTER * PEERS * C
TOK, D, H = 128, 4608, 128
ROWS = D // DEVICES
SHARD = D // (PEERS * C)
SLAB = SHARD + 16
HALF = D // C
PART = HALF // INTER
CHUNK = 512
BF16, F16, F32 = jnp.bfloat16, jnp.float16, jnp.float32
VMEM = pl.BlockSpec(memory_space=pltpu.VMEM)
MIB = 1024 * 1024


def row_terms(x_ref, far_ref, cot_ref, far_cot_ref, half_ref, inv_ref, all_ref):
    def inverse(ref):
        square = jnp.zeros((TOK, 128), F32)
        for at in range(0, D, 128):
            wide = ref[:, at : at + 128].astype(F32)
            square += wide * wide
        return lax.rsqrt(jnp.sum(square, axis=1, keepdims=True) * (1.0 / D) + EPS)

    inv = inverse(x_ref)
    inv_ref[...] = jnp.broadcast_to(inv, (TOK, 128))
    near, far = cot_ref[...].astype(F32), far_cot_ref[...].astype(F32)
    largest = jnp.max(jnp.maximum(jnp.abs(near), jnp.abs(far)), axis=(0, 1), keepdims=True)
    power = jnp.ceil(jnp.log2(jnp.maximum(largest, 1e-30)))
    scale = jnp.exp2(-power)
    scaled = jnp.concatenate([near * (inv * scale), far * (inverse(far_ref) * scale)], axis=0)
    high = scaled.astype(BF16)
    low = (scaled - high.astype(F32)).astype(BF16)
    both = jnp.concatenate([high, low], axis=1)
    for at in range(0, D, CHUNK):
        turned = jnp.concatenate([x_ref[:, at : at + CHUNK].T, far_ref[:, at : at + CHUNK].T], axis=1)
        pair = jnp.dot(turned, both, preferred_element_type=F32)
        all_ref[at : at + CHUNK, :] = pair[:, :H] + pair[:, H:]
    mine = lax.axis_index("core")
    for group in range(INTER):
        for row in range(ROWS):
            start = group * C * PART + row
            to = slice(row * PEERS, (row + 1) * PEERS)
            half_ref[group, to, :] = all_ref[pl.ds(start + mine * ROWS, PEERS, stride=C * ROWS), :]
        half_ref[group, PART:, :] = jnp.broadcast_to(power, (8, H))


def group_sum(parts_ref, out_ref, sum_ref):
    total = jnp.zeros((PART, H), F32)
    for group in range(INTER):
        total += parts_ref[group, :PART] * jnp.exp2(parts_ref[group, PART : PART + 1, :])
    sum_ref[:PART, :] = total
    sum_ref[PART:, :] = jnp.zeros((8 * PEERS - PART, H), F32)
    for peer in range(PEERS):
        out_ref[peer] = sum_ref[pl.ds(peer, 8, stride=PEERS), :]


def input_side(x_ref, cot_ref, inv_ref, own_ref, other_ref, grad_ref, rows_ref, gains_ref, w_ref, g_ref, sg_ref, win_ref):
    mine, my_y, my_zh = lax.axis_index("core"), lax.axis_index("y"), lax.axis_index("zh")
    for hop in range(Y // 2):
        base_y = lax.rem(my_y + Y - 2 * hop, Y)
        for side in range(2):
            from_y = base_y if side == 0 else base_y + 1 - 2 * lax.rem(base_y, 2)
            for turn in range(ZH):
                peer = lax.rem(my_zh + ZH - turn, ZH) * Y + from_y
                for ref, core in ((own_ref, mine), (other_ref, 1 - mine)):
                    shard = 2 * peer + core
                    w_ref[pl.ds(pl.multiple_of(shard * SHARD, SHARD), SHARD), :] = ref[hop, side, turn, :SHARD, :]
                    g_ref[lax.rem(shard, 4), pl.ds(shard // 4, 1), :] = ref[hop, side, turn, SHARD:, :].astype(F32)[:1]
    w_ref[D:, :] = jnp.zeros((32, H), BF16)
    lane = lax.broadcasted_iota(jnp.int32, (16, 128), 1)
    g0, g1, g2, g3 = g_ref[0], g_ref[1], g_ref[2], g_ref[3]
    tiles = (
        jnp.where(lane < 96, g0, pltpu.roll(g1, 96, 1)),
        jnp.where(lane < 64, pltpu.roll(g1, 96, 1), pltpu.roll(g2, 64, 1)),
        jnp.where(lane < 32, pltpu.roll(g2, 64, 1), pltpu.roll(g3, 32, 1)),
    )
    first = ((lax.axis_index("x") * ZL + lax.axis_index("zl")) * PEERS + my_zh * Y + my_y) * C
    first = (first + mine) * ROWS
    base = pl.multiple_of(first // 16 * 16, 16)
    win_ref[:32, :] = w_ref[pl.ds(base, 32), :].astype(F32)
    rows_ref[...] = win_ref[pl.ds(first - base, 8), :]
    wanted = first + lax.broadcasted_iota(jnp.int32, (8, 128), 0)
    column = lax.broadcasted_iota(jnp.int32, (8, 128), 1)
    found = jnp.zeros((8, 128), F32)
    centre = jnp.zeros((TOK, 128), F32)
    inv = inv_ref[...]
    cot = cot_ref[...]
    for at in range(0, D, CHUNK):
        grad = lax.dot_general(cot, w_ref[at : at + CHUNK, :], (((1,), (1,)), ((), ())), preferred_element_type=F32)
        for tile in range(CHUNK // 128):
            here = at + tile * 128
            number = here // 128
            gain = tiles[number % 3][number // 3 : number // 3 + 1, :]
            found += jnp.where(column + here == wanted, gain, 0.0)
            scaled = grad[:, tile * 128 : tile * 128 + 128] * gain
            sg_ref[:, here : here + 128] = scaled
            centre += scaled * (x_ref[:, here : here + 128].astype(F32) * inv)
    gains_ref[...] = jnp.broadcast_to(jnp.sum(found, axis=1, keepdims=True), (8, 128))
    mean = jnp.broadcast_to(jnp.sum(centre, axis=1, keepdims=True) * (1.0 / D), (TOK, 128))
    for here in range(0, D, 128):
        normal = x_ref[:, here : here + 128].astype(F32) * inv
        grad_ref[:, here : here + 128] = (inv * (sg_ref[:, here : here + 128] - normal * mean)).astype(BF16)


def last_sum(parts_ref, rows_ref, gains_ref, weight_ref, gain_ref):
    total = parts_ref[0]
    for peer in range(1, PEERS):
        total += parts_ref[peer]
    total = total * (1.0 / DEVICES)
    weight_ref[...] = (total * gains_ref[...])[:ROWS]
    gain_ref[...] = jnp.broadcast_to(jnp.sum(total * rows_ref[...], axis=1, keepdims=True), (8, 128))


def call(body, outs, scratch=(), flops=0, moved=0):
    return pl.pallas_call(
        body,
        out_shape=[jax.ShapeDtypeStruct(*o) for o in outs],
        scratch_shapes=list(scratch),
        compiler_params=pltpu.CompilerParams(vmem_limit_bytes=40 * MIB),
        cost_estimate=pl.CostEstimate(flops=flops, bytes_accessed=moved, transcendentals=0),
    )


def swap_cores(a):
    return lax.ppermute(a, "core", [(0, 1), (1, 0)])


def shift(a, axis, n, by):
    return lax.ppermute(a, axis, [(i, (i + by) % n) for i in range(n)])


def gathered(slab):
    column = jnp.stack([slab] + [shift(slab, "zh", ZH, turn) for turn in range(1, ZH)])
    two = jnp.stack([column, lax.ppermute(column, "y", [(i, i ^ 1) for i in range(Y)])])
    return jnp.stack([two] + [shift(two, "y", Y, 2 * hop) for hop in range(1, Y // 2)])


def on_device(layer_input, norm_gain, kv_weight, kv_cotangent):
    far, far_cot = swap_cores(layer_input), swap_cores(kv_cotangent)
    gains = jnp.broadcast_to(jnp.pad(norm_gain, (0, 128 - SHARD))[None], (16, 128))
    own = gathered(jnp.concatenate([kv_weight, gains], axis=0))
    other = swap_cores(own)

    half, inv = call(
        row_terms,
        [((INTER, PART + 8, H), F32), ((TOK, 128), F32)],
        [pltpu.VMEM((D, H), F32)],
        flops=4 * TOK * D * H * 2,
        moved=4 * TOK * D + 2 * D * H,
    )(layer_input, far, kv_cotangent, far_cot)
    parts = lax.all_to_all(half.astype(F16), ("x", "zl"), split_axis=0, concat_axis=0, tiled=True).astype(F32)
    (sums,) = call(group_sum, [((PEERS, 8, H), F32)], [pltpu.VMEM((8 * PEERS, H), F32)], flops=INTER * PART * H, moved=4 * HALF * H)(parts)
    last = lax.all_to_all(sums, ("zh", "y"), split_axis=0, concat_axis=0, tiled=True)

    input_grad, rows, row_gains = call(
        input_side,
        [((TOK, D), BF16), ((8, H), F32), ((8, H), F32)],
        [
            pltpu.VMEM((D + 32, H), BF16),
            pltpu.VMEM((4, 16, 128), F32),
            pltpu.VMEM((TOK, D), F32),
            pltpu.VMEM((32 + 8, H), F32),
        ],
        flops=2 * TOK * D * H,
        moved=4 * TOK * D,
    )(layer_input, kv_cotangent, inv, own, other)
    weight_grad, gain_grad = call(last_sum, [((ROWS, H), F32), ((8, 128), F32)], flops=PEERS * 1024, moved=PEERS * 4096)(
        last, rows, row_gains
    )
    return input_grad, weight_grad, gain_grad[:ROWS, 0]


def solution(mesh):
    axes = ("x", "zl", "zh", "y", "core")
    fine = Mesh(mesh.devices.reshape(X, ZL, ZH, Y, C), axes)
    intra = ("zh", "y", "core")
    return jax.shard_map(
        on_device,
        mesh=fine,
        in_specs=(P(axes, None), P(intra), P(intra, None), P(axes, None)),
        out_specs=(P(axes, None), P(axes, None), P(axes)),
        check_vma=False,
    )
```

```python
import jax
import jax.numpy as jnp
from jax import lax
from jax.experimental import pallas as pl
from jax.experimental.pallas import tpu as pltpu
from jax.sharding import Mesh, PartitionSpec as P

EPS = 1e-05
X, ZL, ZH, Y, C = 4, 4, 3, 8, 2
INTER, PEERS = X * ZL, ZH * Y
DEVICES = INTER * PEERS * C
TOK, D, H = 128, 4608, 128
ROWS = D // DEVICES
SHARD = D // (PEERS * C)
SLAB = SHARD + 16
HALF = D // C
PART = HALF // INTER
CHUNK = 512
BF16, F16, F32 = jnp.bfloat16, jnp.float16, jnp.float32
VMEM = pl.BlockSpec(memory_space=pltpu.VMEM)
MIB = 1024 * 1024


def inverse(ref):
    square = jnp.zeros((TOK, 128), F32)
    for at in range(0, D, 128):
        wide = ref[:, at : at + 128].astype(F32)
        square += wide * wide
    return lax.rsqrt(jnp.sum(square, axis=1, keepdims=True) * (1.0 / D) + EPS)


def products(x_ref, scaled, all_ref):
    high = scaled.astype(BF16)
    low = (scaled - high.astype(F32)).astype(BF16)
    both = jnp.concatenate([high, low], axis=1)
    for at in range(0, D, CHUNK):
        pair = jnp.dot(x_ref[:, at : at + CHUNK].T, both, preferred_element_type=F32)
        all_ref[at : at + CHUNK, :] = pair[:, :H] + pair[:, H:]


def rows_of(all_ref, group, row, core):
    return all_ref[pl.ds(group * C * PART + row + core * ROWS, PEERS, stride=C * ROWS), :]


def near_terms(x_ref, cot_ref, half_ref, inv_ref, all_ref):
    inv = inverse(x_ref)
    inv_ref[...] = jnp.broadcast_to(inv, (TOK, 128))
    products(x_ref, cot_ref[...].astype(F32) * inv, all_ref)
    mine = lax.axis_index("core")
    for group in range(INTER):
        for row in range(ROWS):
            half_ref[group, row * PEERS : (row + 1) * PEERS, :] = rows_of(all_ref, group, row, mine)


def far_terms(x_ref, cot_ref, near_cot_ref, near_ref, half_ref, all_ref):
    cot = cot_ref[...].astype(F32)
    largest = jnp.max(jnp.maximum(jnp.abs(cot), jnp.abs(near_cot_ref[...].astype(F32))), axis=(0, 1), keepdims=True)
    power = jnp.ceil(jnp.log2(jnp.maximum(largest, 1e-30)))
    scale = jnp.exp2(-power)
    products(x_ref, cot * (inverse(x_ref) * scale), all_ref)
    mine = lax.axis_index("core")
    for group in range(INTER):
        for row in range(ROWS):
            to = slice(row * PEERS, (row + 1) * PEERS)
            half_ref[group, to, :] = rows_of(all_ref, group, row, mine) + near_ref[group, to, :] * scale
        half_ref[group, PART:, :] = jnp.broadcast_to(power, (8, H))


def group_sum(parts_ref, out_ref, sum_ref):
    total = jnp.zeros((PART, H), F32)
    for group in range(INTER):
        total += parts_ref[group, :PART] * jnp.exp2(parts_ref[group, PART : PART + 1, :])
    sum_ref[:PART, :] = total
    sum_ref[PART:, :] = jnp.zeros((8 * PEERS - PART, H), F32)
    for peer in range(PEERS):
        out_ref[peer] = sum_ref[pl.ds(peer, 8, stride=PEERS), :]


def outputs(x_ref, cot_ref, inv_ref, own_ref, other_ref, total_ref, grad_ref, weight_ref, gain_ref, w_ref, g_ref, sg_ref, win_ref):
    mine, my_y, my_zh = lax.axis_index("core"), lax.axis_index("y"), lax.axis_index("zh")
    for hop in range(Y // 2):
        base_y = lax.rem(my_y + Y - 2 * hop, Y)
        for side in range(2):
            from_y = base_y if side == 0 else base_y + 1 - 2 * lax.rem(base_y, 2)
            for turn in range(ZH):
                peer = lax.rem(my_zh + ZH - turn, ZH) * Y + from_y
                for ref, core in ((own_ref, mine), (other_ref, 1 - mine)):
                    shard = 2 * peer + core
                    w_ref[pl.ds(pl.multiple_of(shard * SHARD, SHARD), SHARD), :] = ref[hop, side, turn, :SHARD, :]
                    g_ref[lax.rem(shard, 4), pl.ds(shard // 4, 1), :] = ref[hop, side, turn, SHARD:, :].astype(F32)[:1]
    w_ref[D:, :] = jnp.zeros((32, H), BF16)
    lane = lax.broadcasted_iota(jnp.int32, (16, 128), 1)
    g0, g1, g2, g3 = g_ref[0], g_ref[1], g_ref[2], g_ref[3]
    tiles = (
        jnp.where(lane < 96, g0, pltpu.roll(g1, 96, 1)),
        jnp.where(lane < 64, pltpu.roll(g1, 96, 1), pltpu.roll(g2, 64, 1)),
        jnp.where(lane < 32, pltpu.roll(g2, 64, 1), pltpu.roll(g3, 32, 1)),
    )
    first = ((lax.axis_index("x") * ZL + lax.axis_index("zl")) * PEERS + my_zh * Y + my_y) * C
    first = (first + mine) * ROWS
    base = pl.multiple_of(first // 16 * 16, 16)
    win_ref[:32, :] = w_ref[pl.ds(base, 32), :].astype(F32)
    wanted = first + lax.broadcasted_iota(jnp.int32, (8, 128), 0)
    column = lax.broadcasted_iota(jnp.int32, (8, 128), 1)
    found = jnp.zeros((8, 128), F32)
    centre = jnp.zeros((TOK, 128), F32)
    inv = inv_ref[...]
    cot = cot_ref[...]
    for at in range(0, D, CHUNK):
        grad = lax.dot_general(cot, w_ref[at : at + CHUNK, :], (((1,), (1,)), ((), ())), preferred_element_type=F32)
        for tile in range(CHUNK // 128):
            here = at + tile * 128
            number = here // 128
            gain = tiles[number % 3][number // 3 : number // 3 + 1, :]
            found += jnp.where(column + here == wanted, gain, 0.0)
            scaled = grad[:, tile * 128 : tile * 128 + 128] * gain
            sg_ref[:, here : here + 128] = scaled
            centre += scaled * (x_ref[:, here : here + 128].astype(F32) * inv)
    total = total_ref[...]
    weight_ref[...] = (total * jnp.sum(found, axis=1, keepdims=True))[:ROWS]
    gain_ref[...] = jnp.sum((total * win_ref[pl.ds(first - base, 8), :]).T, axis=0)[:ROWS]
    mean = jnp.broadcast_to(jnp.sum(centre, axis=1, keepdims=True) * (1.0 / D), (TOK, 128))
    for here in range(0, D, 128):
        normal = x_ref[:, here : here + 128].astype(F32) * inv
        grad_ref[:, here : here + 128] = (inv * (sg_ref[:, here : here + 128] - normal * mean)).astype(BF16)


def last_sum(parts_ref, total_ref):
    total = parts_ref[0]
    for peer in range(1, PEERS):
        total += parts_ref[peer]
    total_ref[...] = total * (1.0 / DEVICES)


def call(body, outs, scratch=(), flops=0, moved=0):
    return pl.pallas_call(
        body,
        out_shape=[jax.ShapeDtypeStruct(*o) for o in outs],
        scratch_shapes=list(scratch),
        compiler_params=pltpu.CompilerParams(vmem_limit_bytes=40 * MIB),
        cost_estimate=pl.CostEstimate(flops=flops, bytes_accessed=moved, transcendentals=0),
    )


def swap_cores(a):
    return lax.ppermute(a, "core", [(0, 1), (1, 0)])


def shift(a, axis, n, by):
    return lax.ppermute(a, axis, [(i, (i + by) % n) for i in range(n)])


def on_device(layer_input, norm_gain, kv_weight, kv_cotangent):
    barrier = lax.optimization_barrier
    far, far_cot = swap_cores(layer_input), swap_cores(kv_cotangent)
    gains = jnp.broadcast_to(jnp.pad(norm_gain, (0, 128 - SHARD))[None], (16, 128))
    slab = jnp.concatenate([kv_weight, gains], axis=0)
    turns = [shift(slab, "zh", ZH, turn) for turn in range(1, ZH)]
    near, inv = call(
        near_terms,
        [((INTER, PART, H), F32), ((TOK, 128), F32)],
        [pltpu.VMEM((D, H), F32)],
        flops=4 * TOK * D * H,
        moved=2 * TOK * D + 2 * D * H,
    )(layer_input, kv_cotangent)
    turns, near = barrier((turns, near))
    column = jnp.stack([slab] + turns)
    beside = lax.ppermute(column, "y", [(i, i ^ 1) for i in range(Y)])
    far, column = barrier((far, column))
    (half,) = call(
        far_terms,
        [((INTER, PART + 8, H), F32)],
        [pltpu.VMEM((D, H), F32)],
        flops=4 * TOK * D * H,
        moved=2 * TOK * D + 4 * D * H,
    )(far, far_cot, kv_cotangent, near)
    short = half.astype(F16)
    beside, short = barrier((beside, short))
    parts = lax.all_to_all(short, ("x", "zl"), split_axis=0, concat_axis=0, tiled=True).astype(F32)
    two = jnp.stack([column, beside])
    hops = [shift(two, "y", Y, 2 * hop) for hop in range(1, Y // 2)]
    (sums,) = call(group_sum, [((PEERS, 8, H), F32)], [pltpu.VMEM((8 * PEERS, H), F32)], flops=INTER * PART * H, moved=4 * HALF * H)(parts)
    last = lax.all_to_all(sums, ("zh", "y"), split_axis=0, concat_axis=0, tiled=True)
    hops, _ = barrier((hops, sums))
    own = jnp.stack([two] + hops)
    other = swap_cores(own)

    (total,) = call(last_sum, [((8, H), F32)], flops=int(2e10), moved=PEERS * 4096)(last)
    return call(
        outputs,
        [((TOK, D), BF16), ((ROWS, H), F32), ((ROWS,), F32)],
        [
            pltpu.VMEM((D + 32, H), BF16),
            pltpu.VMEM((4, 16, 128), F32),
            pltpu.VMEM((TOK, D), F32),
            pltpu.VMEM((32 + 8, H), F32),
        ],
        flops=2 * TOK * D * H,
        moved=4 * TOK * D,
    )(layer_input, kv_cotangent, inv, own, other, total)


def solution(mesh):
    axes = ("x", "zl", "zh", "y", "core")
    fine = Mesh(mesh.devices.reshape(X, ZL, ZH, Y, C), axes)
    intra = ("zh", "y", "core")
    return jax.shard_map(
        on_device,
        mesh=fine,
        in_specs=(P(axes, None), P(intra), P(intra, None), P(axes, None)),
        out_specs=(P(axes, None), P(axes, None), P(axes)),
        check_vma=False,
    )
```

```python
import jax
import jax.numpy as jnp
from jax import lax
from jax.experimental import pallas as pl
from jax.experimental.pallas import tpu as pltpu
from jax.sharding import Mesh, PartitionSpec as P

EPS = 1e-05
X, ZL, ZH, Y, C = 4, 4, 3, 8, 2
PLANE, LINE = X * Y, ZL * ZH
DEVICES = PLANE * LINE * C
TOK, D, H = 128, 4608, 128
ROWS = D // DEVICES
SHARD = D // (ZH * Y * C)
SLAB = SHARD + 16
HALF = D // C
PART = HALF // PLANE
CHUNK = 512
BF16, F16, F32 = jnp.bfloat16, jnp.float16, jnp.float32
VMEM = pl.BlockSpec(memory_space=pltpu.VMEM)
MIB = 1024 * 1024


def inverse(ref):
    square = jnp.zeros((TOK, 128), F32)
    for at in range(0, D, 128):
        wide = ref[:, at : at + 128].astype(F32)
        square += wide * wide
    return lax.rsqrt(jnp.sum(square, axis=1, keepdims=True) * (1.0 / D) + EPS)


def products(x_ref, scaled, all_ref):
    high = scaled.astype(BF16)
    low = (scaled - high.astype(F32)).astype(BF16)
    both = jnp.concatenate([high, low], axis=1)
    for at in range(0, D, CHUNK):
        pair = jnp.dot(x_ref[:, at : at + CHUNK].T, both, preferred_element_type=F32)
        all_ref[at : at + CHUNK, :] = pair[:, :H] + pair[:, H:]


def rows_of(all_ref, chip, row, core, first, count):
    start = chip // Y * (D // X) + chip % Y * (C * ROWS) + row + first * SHARD
    return all_ref[pl.ds(start + core * ROWS, count, stride=SHARD), :]


def pieces():
    for row in range(ROWS):
        for first, count in ((0, 8), (8, 4)) if row % 2 == 0 else ((0, 4), (4, 8)):
            yield row, first, count, row * LINE + first


def near_terms(x_ref, cot_ref, half_ref, inv_ref, all_ref):
    inv = inverse(x_ref)
    inv_ref[...] = jnp.broadcast_to(inv, (TOK, 128))
    products(x_ref, cot_ref[...].astype(F32) * inv, all_ref)
    mine = lax.axis_index("core")
    for chip in range(PLANE):
        for row, first, count, at in pieces():
            half_ref[chip, at : at + count, :] = rows_of(all_ref, chip, row, mine, first, count)


def far_terms(x_ref, cot_ref, near_cot_ref, near_ref, half_ref, all_ref):
    cot = cot_ref[...].astype(F32)
    largest = jnp.max(jnp.maximum(jnp.abs(cot), jnp.abs(near_cot_ref[...].astype(F32))), axis=(0, 1), keepdims=True)
    power = jnp.ceil(jnp.log2(jnp.maximum(largest, 1e-30)))
    scale = jnp.exp2(-power)
    products(x_ref, cot * (inverse(x_ref) * scale), all_ref)
    mine = lax.axis_index("core")
    for chip in range(PLANE):
        for row, first, count, at in pieces():
            to = slice(at, at + count)
            half_ref[chip, to, :] = rows_of(all_ref, chip, row, mine, first, count) + near_ref[chip, to, :] * scale
        half_ref[chip, PART:, :] = jnp.broadcast_to(power, (8, H))


def plane_sum(parts_ref, out_ref, sum_ref):
    total = jnp.zeros((PART, H), F32)
    for chip in range(PLANE):
        total += parts_ref[chip, :PART] * jnp.exp2(parts_ref[chip, PART : PART + 1, :])
    sum_ref[:PART, :] = total
    sum_ref[PART:, :] = jnp.zeros((8 * LINE - PART, H), F32)
    for place in range(LINE):
        out_ref[place] = sum_ref[pl.ds(place, 8, stride=LINE), :]


def outputs(x_ref, cot_ref, inv_ref, own_ref, other_ref, total_ref, grad_ref, weight_ref, gain_ref, w_ref, g_ref, sg_ref, win_ref):
    mine, my_y, my_zh = lax.axis_index("core"), lax.axis_index("y"), lax.axis_index("zh")
    for turn in range(ZH):
        from_zh = lax.rem(my_zh + ZH - turn, ZH)
        for y in range(Y):
            for ref, core in ((own_ref, mine), (other_ref, 1 - mine)):
                shard = 2 * (from_zh * Y + y) + core
                w_ref[pl.ds(pl.multiple_of(shard * SHARD, SHARD), SHARD), :] = ref[turn, y, :SHARD, :]
                g_ref[lax.rem(shard, 4), pl.ds(shard // 4, 1), :] = ref[turn, y, SHARD:, :].astype(F32)[:1]
    w_ref[D:, :] = jnp.zeros((32, H), BF16)
    lane = lax.broadcasted_iota(jnp.int32, (16, 128), 1)
    g0, g1, g2, g3 = g_ref[0], g_ref[1], g_ref[2], g_ref[3]
    tiles = (
        jnp.where(lane < 96, g0, pltpu.roll(g1, 96, 1)),
        jnp.where(lane < 64, pltpu.roll(g1, 96, 1), pltpu.roll(g2, 64, 1)),
        jnp.where(lane < 32, pltpu.roll(g2, 64, 1), pltpu.roll(g3, 32, 1)),
    )
    first = ((lax.axis_index("x") * ZL + lax.axis_index("zl")) * (ZH * Y) + my_zh * Y + my_y) * C
    first = (first + mine) * ROWS
    base = pl.multiple_of(first // 16 * 16, 16)
    win_ref[:32, :] = w_ref[pl.ds(base, 32), :].astype(F32)
    wanted = first + lax.broadcasted_iota(jnp.int32, (8, 128), 0)
    column = lax.broadcasted_iota(jnp.int32, (8, 128), 1)
    found = jnp.zeros((8, 128), F32)
    centre = jnp.zeros((TOK, 128), F32)
    inv = inv_ref[...]
    cot = cot_ref[...]
    for at in range(0, D, CHUNK):
        grad = lax.dot_general(cot, w_ref[at : at + CHUNK, :], (((1,), (1,)), ((), ())), preferred_element_type=F32)
        for tile in range(CHUNK // 128):
            here = at + tile * 128
            number = here // 128
            gain = tiles[number % 3][number // 3 : number // 3 + 1, :]
            found += jnp.where(column + here == wanted, gain, 0.0)
            scaled = grad[:, tile * 128 : tile * 128 + 128] * gain
            sg_ref[:, here : here + 128] = scaled
            centre += scaled * (x_ref[:, here : here + 128].astype(F32) * inv)
    total = total_ref[...]
    weight_ref[...] = (total * jnp.sum(found, axis=1, keepdims=True))[:ROWS]
    gain_ref[...] = jnp.sum((total * win_ref[pl.ds(first - base, 8), :]).T, axis=0)[:ROWS]
    mean = jnp.broadcast_to(jnp.sum(centre, axis=1, keepdims=True) * (1.0 / D), (TOK, 128))
    for here in range(0, D, 128):
        normal = x_ref[:, here : here + 128].astype(F32) * inv
        grad_ref[:, here : here + 128] = (inv * (sg_ref[:, here : here + 128] - normal * mean)).astype(BF16)


def last_sum(parts_ref, total_ref):
    total = parts_ref[0]
    for place in range(1, LINE):
        total += parts_ref[place]
    total_ref[...] = total * (1.0 / DEVICES)


def call(body, outs, scratch=(), flops=0, moved=0):
    return pl.pallas_call(
        body,
        out_shape=[jax.ShapeDtypeStruct(*o) for o in outs],
        scratch_shapes=list(scratch),
        compiler_params=pltpu.CompilerParams(vmem_limit_bytes=40 * MIB),
        cost_estimate=pl.CostEstimate(flops=flops, bytes_accessed=moved, transcendentals=0),
    )


def swap_cores(a):
    return lax.ppermute(a, "core", [(0, 1), (1, 0)])


def exchange(a, axis):
    return lax.all_to_all(a, axis, split_axis=0, concat_axis=0, tiled=True)


def shift(a, axis, n, by):
    return lax.ppermute(a, axis, [(i, (i + by) % n) for i in range(n)])


def on_device(layer_input, norm_gain, kv_weight, kv_cotangent):
    far, far_cot = swap_cores(layer_input), swap_cores(kv_cotangent)
    gains = jnp.broadcast_to(jnp.pad(norm_gain, (0, 128 - SHARD))[None], (16, 128))
    slab = jnp.concatenate([kv_weight, gains], axis=0)
    column = exchange(jnp.broadcast_to(slab[None], (Y, SLAB, H)), "y")
    turns = [shift(column, "zh", ZH, turn) for turn in range(1, ZH)]
    near, inv = call(
        near_terms,
        [((PLANE, PART, H), F32), ((TOK, 128), F32)],
        [pltpu.VMEM((D, H), F32)],
        flops=4 * TOK * D * H,
        moved=2 * TOK * D + 2 * D * H,
    )(layer_input, kv_cotangent)
    (half,) = call(
        far_terms,
        [((PLANE, PART + 8, H), F32)],
        [pltpu.VMEM((D, H), F32)],
        flops=4 * TOK * D * H,
        moved=2 * TOK * D + 4 * D * H,
    )(far, far_cot, kv_cotangent, near)
    parts = exchange(half.astype(F16), ("x", "y")).astype(F32)
    (sums,) = call(plane_sum, [((LINE, 8, H), F32)], [pltpu.VMEM((8 * LINE, H), F32)], flops=PLANE * PART * H, moved=4 * HALF * H)(parts)
    last = exchange(sums, ("zl", "zh"))
    turns, _ = lax.optimization_barrier((turns, sums))
    own = jnp.stack([column] + turns)
    other = swap_cores(own)

    (total,) = call(last_sum, [((8, H), F32)], flops=int(2e10), moved=LINE * 4096)(last)
    return call(
        outputs,
        [((TOK, D), BF16), ((ROWS, H), F32), ((ROWS,), F32)],
        [
            pltpu.VMEM((D + 32, H), BF16),
            pltpu.VMEM((4, 16, 128), F32),
            pltpu.VMEM((TOK, D), F32),
            pltpu.VMEM((32 + 8, H), F32),
        ],
        flops=2 * TOK * D * H,
        moved=4 * TOK * D,
    )(layer_input, kv_cotangent, inv, own, other, total)


def solution(mesh):
    axes = ("x", "zl", "zh", "y", "core")
    fine = Mesh(mesh.devices.reshape(X, ZL, ZH, Y, C), axes)
    intra = ("zh", "y", "core")
    return jax.shard_map(
        on_device,
        mesh=fine,
        in_specs=(P(axes, None), P(intra), P(intra, None), P(axes, None)),
        out_specs=(P(axes, None), P(axes, None), P(axes)),
        check_vma=False,
    )
```

```python
import jax
import jax.numpy as jnp
from jax import lax
from jax.experimental import pallas as pl
from jax.experimental.pallas import tpu as pltpu
from jax.sharding import Mesh, PartitionSpec as P

EPS = 1e-05
X, ZL, ZH, Y, C = 4, 4, 3, 8, 2
PLANE, LINE = X * Y, ZL * ZH
DEVICES = PLANE * LINE * C
TOK, D, H = 128, 4608, 128
ROWS = D // DEVICES
SHARD = D // (ZH * Y * C)

SLAB = SHARD + 16
HALF = D // C
PART = HALF // PLANE
PADDED = PART + 8
SIDE = LINE * Y
CHUNK = 512
BF16, F16, F32 = jnp.bfloat16, jnp.float16, jnp.float32
VMEM = pl.BlockSpec(memory_space=pltpu.VMEM)
MIB = 1024 * 1024

def make_slabs(w_ref, gain_ref, slabs_ref, gain_row, sem):
    fetch = pltpu.make_async_copy(gain_ref, gain_row, sem.at[Y])
    fetch.start()
    copies = [pltpu.make_async_copy(w_ref, slabs_ref.at[y, :SHARD, :], sem.at[y]) for y in range(Y)]
    for copy in copies:
        copy.start()
    fetch.wait()
    gains = jnp.broadcast_to(gain_row[...].astype(F32), (16, SHARD)).astype(BF16)
    for y in range(Y):
        slabs_ref[y, SHARD:, :] = jnp.zeros((16, H), BF16)
        slabs_ref[y, SHARD:, :SHARD] = gains
    for copy in copies:
        copy.wait()

def inverse(ref):
    square = jnp.zeros((TOK, 128), F32)
    for at in range(0, D, 128):
        wide = ref[:, at : at + 128].astype(F32)
        square += wide * wide
    return lax.rsqrt(jnp.sum(square, axis=1, keepdims=True) * (1.0 / D) + EPS)

def products(x_ref, scaled, all_ref):
    high = scaled.astype(BF16)
    low = (scaled - high.astype(F32)).astype(BF16)
    both = jnp.concatenate([high, low], axis=1)
    for at in range(0, D, CHUNK):
        pair = jnp.dot(x_ref[:, at : at + CHUNK].T, both, preferred_element_type=F32)
        all_ref[at : at + CHUNK, :] = pair[:, :H] + pair[:, H:]

def near_terms(x_ref, cot_ref, half_ref, inv_ref, all_ref):
    inv = inverse(x_ref)
    inv_ref[...] = jnp.broadcast_to(inv, (TOK, 128))
    products(x_ref, cot_ref[...].astype(F32) * inv, all_ref)
    mine = lax.axis_index("core")
    for x in range(X):
        for row in range(ROWS):
            at = (x * ROWS + row) * SIDE
            half_ref[at : at + SIDE, :] = all_ref[pl.ds(x * (D // X) + row + mine * ROWS, SIDE, stride=C * ROWS), :]

def far_terms(x_ref, cot_ref, near_cot_ref, near_ref, half_ref, all_ref):
    cot = cot_ref[...].astype(F32)
    largest = jnp.max(jnp.maximum(jnp.abs(cot), jnp.abs(near_cot_ref[...].astype(F32))), axis=(0, 1), keepdims=True)
    power = jnp.ceil(jnp.log2(jnp.maximum(largest, 1e-30)))
    scale = jnp.exp2(-power)
    products(x_ref, cot * (inverse(x_ref) * scale), all_ref)
    mine = lax.axis_index("core")
    for x in range(X):
        for row in range(ROWS):
            for place in range(LINE):
                start = x * (D // X) + place * SHARD + row + mine * ROWS
                at = (x * ROWS + row) * SIDE + place * Y
                total = all_ref[pl.ds(start, Y, stride=C * ROWS), :] + near_ref[at : at + Y, :] * scale
                half_ref[pl.ds(x * Y * PADDED + row * LINE + place, Y, stride=PADDED), :] = total
    for chip in range(PLANE):
        half_ref[chip * PADDED + PART : (chip + 1) * PADDED, :] = jnp.broadcast_to(power, (8, H))

def plane_sum(parts_ref, out_ref, sum_ref):
    total = jnp.zeros((PART, H), F32)
    for chip in range(PLANE):
        total += parts_ref[chip, :PART] * jnp.exp2(parts_ref[chip, PART : PART + 1, :])
    sum_ref[:PART, :] = total
    sum_ref[PART:, :] = jnp.zeros((8 * LINE - PART, H), F32)
    for place in range(LINE):
        out_ref[place] = sum_ref[pl.ds(place, 8, stride=LINE), :]

def outputs(x_ref, cot_ref, inv_ref, own_ref, other_ref, total_ref, grad_ref, weight_ref, gain_ref, w_ref, g_ref, sg_ref, win_ref):
    mine, my_y, my_zh = lax.axis_index("core"), lax.axis_index("y"), lax.axis_index("zh")
    for turn in range(ZH):
        from_zh = lax.rem(my_zh + ZH - turn, ZH)
        for y in range(Y):
            for ref, core in ((own_ref, mine), (other_ref, 1 - mine)):
                shard = 2 * (from_zh * Y + y) + core
                w_ref[pl.ds(pl.multiple_of(shard * SHARD, SHARD), SHARD), :] = ref[turn, y, :SHARD, :]
                g_ref[lax.rem(shard, 4), pl.ds(shard // 4, 1), :] = ref[turn, y, SHARD:, :].astype(F32)[:1]
    w_ref[D:, :] = jnp.zeros((32, H), BF16)
    lane = lax.broadcasted_iota(jnp.int32, (16, 128), 1)
    g0, g1, g2, g3 = g_ref[0], g_ref[1], g_ref[2], g_ref[3]
    tiles = (
        jnp.where(lane < 96, g0, pltpu.roll(g1, 96, 1)),
        jnp.where(lane < 64, pltpu.roll(g1, 96, 1), pltpu.roll(g2, 64, 1)),
        jnp.where(lane < 32, pltpu.roll(g2, 64, 1), pltpu.roll(g3, 32, 1)),
    )
    first = ((lax.axis_index("x") * ZL + lax.axis_index("zl")) * (ZH * Y) + my_zh * Y + my_y) * C
    first = (first + mine) * ROWS
    base = pl.multiple_of(first // 16 * 16, 16)
    win_ref[:32, :] = w_ref[pl.ds(base, 32), :].astype(F32)
    wanted = first + lax.broadcasted_iota(jnp.int32, (8, 128), 0)
    column = lax.broadcasted_iota(jnp.int32, (8, 128), 1)
    found = jnp.zeros((8, 128), F32)
    centre = jnp.zeros((TOK, 128), F32)
    inv = inv_ref[...]
    cot = cot_ref[...]
    for at in range(0, D, CHUNK):
        grad = lax.dot_general(cot, w_ref[at : at + CHUNK, :], (((1,), (1,)), ((), ())), preferred_element_type=F32)
        for tile in range(CHUNK // 128):
            here = at + tile * 128
            number = here // 128
            gain = tiles[number % 3][number // 3 : number // 3 + 1, :]
            found += jnp.where(column + here == wanted, gain, 0.0)
            scaled = grad[:, tile * 128 : tile * 128 + 128] * gain
            sg_ref[:, here : here + 128] = scaled
            centre += scaled * (x_ref[:, here : here + 128].astype(F32) * inv)
    total = total_ref[...]
    weight_ref[...] = (total * jnp.sum(found, axis=1, keepdims=True))[:ROWS]
    gain_ref[...] = jnp.sum((total * win_ref[pl.ds(first - base, 8), :]).T, axis=0)[:ROWS]
    mean = jnp.broadcast_to(jnp.sum(centre, axis=1, keepdims=True) * (1.0 / D), (TOK, 128))
    for here in range(0, D, 128):
        normal = x_ref[:, here : here + 128].astype(F32) * inv
        grad_ref[:, here : here + 128] = (inv * (sg_ref[:, here : here + 128] - normal * mean)).astype(BF16)

def last_sum(parts_ref, total_ref):
    total = parts_ref[0]
    for place in range(1, LINE):
        total += parts_ref[place]
    total_ref[...] = total * (1.0 / DEVICES)

def call(body, outs, scratch=(), flops=0, moved=0, limit=40, **more):
    return pl.pallas_call(
        body,
        **more,
        out_shape=[jax.ShapeDtypeStruct(*o) for o in outs],
        scratch_shapes=list(scratch),
        compiler_params=pltpu.CompilerParams(vmem_limit_bytes=limit * MIB),
        cost_estimate=pl.CostEstimate(flops=flops, bytes_accessed=moved, transcendentals=0),
    )

def swap_cores(a):
    return lax.ppermute(a, "core", [(0, 1), (1, 0)])

def exchange(a, axis):
    return lax.all_to_all(a, axis, split_axis=0, concat_axis=0, tiled=True)

def shift(a, axis, n, by):
    return lax.ppermute(a, axis, [(i, (i + by) % n) for i in range(n)])

def on_device(layer_input, norm_gain, kv_weight, kv_cotangent):
    far, far_cot = swap_cores(layer_input), swap_cores(kv_cotangent)
    hbm = pl.BlockSpec(memory_space=pltpu.HBM)
    (slabs,) = call(
        make_slabs,
        [((Y, SLAB, H), BF16)],
        [pltpu.VMEM((1, SHARD), BF16), pltpu.SemaphoreType.DMA((Y + 1,))],
        flops=int(2e10),
        limit=60,
        in_specs=[hbm, hbm],
    )(kv_weight, norm_gain.reshape(1, SHARD))
    column = exchange(slabs, "y")
    turns = [shift(column, "zh", ZH, turn) for turn in range(1, ZH)]
    near, inv = call(
        near_terms,
        [((HALF, H), F32), ((TOK, 128), F32)],
        [pltpu.VMEM((D, H), F32)],
        flops=4 * TOK * D * H,
        moved=2 * TOK * D + 2 * D * H,
    )(layer_input, kv_cotangent)
    (half,) = call(
        far_terms,
        [((PLANE * PADDED, H), F32)],
        [pltpu.VMEM((D, H), F32)],
        flops=4 * TOK * D * H,
        moved=2 * TOK * D + 4 * D * H,
    )(far, far_cot, kv_cotangent, near)
    parts = exchange(half.astype(F16).reshape(PLANE, PADDED, H), ("x", "y")).astype(F32)
    (sums,) = call(plane_sum, [((LINE, 8, H), F32)], [pltpu.VMEM((8 * LINE, H), F32)], flops=PLANE * PART * H, moved=4 * HALF * H)(parts)
    last = exchange(sums, ("zl", "zh"))
    turns, _ = lax.optimization_barrier((turns, sums))
    own = jnp.stack([column] + turns)
    other = swap_cores(own)

    (total,) = call(last_sum, [((8, H), F32)], flops=int(2e10), moved=LINE * 4096)(last)
    return call(
        outputs,
        [((TOK, D), BF16), ((ROWS, H), F32), ((ROWS,), F32)],
        [
            pltpu.VMEM((D + 32, H), BF16),
            pltpu.VMEM((4, 16, 128), F32),
            pltpu.VMEM((TOK, D), F32),
            pltpu.VMEM((32 + 8, H), F32),
        ],
        flops=2 * TOK * D * H,
        moved=4 * TOK * D,
    )(layer_input, kv_cotangent, inv, own, other, total)

def solution(mesh):
    axes = ("x", "zl", "zh", "y", "core")
    fine = Mesh(mesh.devices.reshape(X, ZL, ZH, Y, C), axes)
    intra = ("zh", "y", "core")
    return jax.shard_map(
        on_device,
        mesh=fine,
        in_specs=(P(axes, None), P(intra), P(intra, None), P(axes, None)),
        out_specs=(P(axes, None), P(axes, None), P(axes)),
        check_vma=False,
    )
```

```python
import jax
import jax.numpy as jnp
from jax import lax
from jax.experimental import pallas as pl
from jax.experimental.pallas import tpu as pltpu
from jax.sharding import Mesh, PartitionSpec as P

EPS = 1e-05
X, ZL, ZH, Y, C = 4, 4, 3, 8, 2
PLANE, LINE = X * Y, ZL * ZH
DEVICES = PLANE * LINE * C
TOK, D, H = 128, 4608, 128
ROWS = D // DEVICES
SHARD = D // (ZH * Y * C)
SLAB = SHARD + 16
HALF = D // C
PART = HALF // PLANE
PADDED = PART + 8
SIDE = LINE * Y
CHUNK = 512
BF16, F16, F32 = jnp.bfloat16, jnp.float16, jnp.float32
VMEM = pl.BlockSpec(memory_space=pltpu.VMEM)
MIB = 1024 * 1024

def make_slabs(w_ref, gain_ref, slabs_ref, slab, gain_row, sem):
    fetches = [
        pltpu.make_async_copy(gain_ref, gain_row, sem.at[Y]),
        pltpu.make_async_copy(w_ref, slab.at[:SHARD, :], sem.at[Y + 1]),
    ]
    for copy in fetches:
        copy.start()
    slab[SHARD:, :] = jnp.zeros((16, H), BF16)
    fetches[0].wait()
    slab[SHARD:, :SHARD] = jnp.broadcast_to(gain_row[...].astype(F32), (16, SHARD)).astype(BF16)
    fetches[1].wait()
    copies = [pltpu.make_async_copy(slab, slabs_ref.at[y], sem.at[y]) for y in range(Y)]
    for copy in copies:
        copy.start()
    for copy in copies:
        copy.wait()


def inverse(ref):
    square = jnp.zeros((TOK, 128), F32)
    for at in range(0, D, 128):
        wide = ref[:, at : at + 128].astype(F32)
        square += wide * wide
    return lax.rsqrt(jnp.sum(square, axis=1, keepdims=True) * (1.0 / D) + EPS)

def products(x_ref, scaled, all_ref):
    high = scaled.astype(BF16)
    low = (scaled - high.astype(F32)).astype(BF16)
    both = jnp.concatenate([high, low], axis=1)
    for at in range(0, D, CHUNK):
        pair = jnp.dot(x_ref[:, at : at + CHUNK].T, both, preferred_element_type=F32)
        all_ref[at : at + CHUNK, :] = pair[:, :H] + pair[:, H:]

def near_terms(x_ref, cot_ref, half_ref, inv_ref, all_ref):
    inv = inverse(x_ref)
    inv_ref[...] = jnp.broadcast_to(inv, (TOK, 128))
    products(x_ref, cot_ref[...].astype(F32) * inv, all_ref)
    mine = lax.axis_index("core")
    for x in range(X):
        for row in range(ROWS):
            at = (x * ROWS + row) * SIDE
            half_ref[at : at + SIDE, :] = all_ref[pl.ds(x * (D // X) + row + mine * ROWS, SIDE, stride=C * ROWS), :]

def far_terms(x_ref, cot_ref, near_cot_ref, near_ref, half_ref, all_ref):
    cot = cot_ref[...].astype(F32)
    largest = jnp.max(jnp.maximum(jnp.abs(cot), jnp.abs(near_cot_ref[...].astype(F32))), axis=(0, 1), keepdims=True)
    power = jnp.ceil(jnp.log2(jnp.maximum(largest, 1e-30)))
    scale = jnp.exp2(-power)
    products(x_ref, cot * (inverse(x_ref) * scale), all_ref)
    mine = lax.axis_index("core")
    for x in range(X):
        for row in range(ROWS):
            for place in range(LINE):
                start = x * (D // X) + place * SHARD + row + mine * ROWS
                at = (x * ROWS + row) * SIDE + place * Y
                total = all_ref[pl.ds(start, Y, stride=C * ROWS), :] + near_ref[at : at + Y, :] * scale
                half_ref[pl.ds(x * Y * PADDED + row * LINE + place, Y, stride=PADDED), :] = total
    for chip in range(PLANE):
        half_ref[chip * PADDED + PART : (chip + 1) * PADDED, :] = jnp.broadcast_to(power, (8, H))

def plane_sum(parts_ref, out_ref, sum_ref):
    total = jnp.zeros((PART, H), F32)
    for chip in range(PLANE):
        total += parts_ref[chip, :PART] * jnp.exp2(parts_ref[chip, PART : PART + 1, :])
    sum_ref[:PART, :] = total
    sum_ref[PART:, :] = jnp.zeros((8 * LINE - PART, H), F32)
    for place in range(LINE):
        out_ref[place] = sum_ref[pl.ds(place, 8, stride=LINE), :]

def outputs(x_ref, cot_ref, inv_ref, own_ref, other_ref, total_ref, grad_ref, weight_ref, gain_ref, w_ref, g_ref, sg_ref, win_ref):
    mine, my_y, my_zh = lax.axis_index("core"), lax.axis_index("y"), lax.axis_index("zh")
    for turn in range(ZH):
        from_zh = lax.rem(my_zh + ZH - turn, ZH)
        for y in range(Y):
            for ref, core in ((own_ref, mine), (other_ref, 1 - mine)):
                shard = 2 * (from_zh * Y + y) + core
                w_ref[pl.ds(pl.multiple_of(shard * SHARD, SHARD), SHARD), :] = ref[turn, y, :SHARD, :]
                g_ref[lax.rem(shard, 4), pl.ds(shard // 4, 1), :] = ref[turn, y, SHARD:, :].astype(F32)[:1]
    w_ref[D:, :] = jnp.zeros((32, H), BF16)
    lane = lax.broadcasted_iota(jnp.int32, (16, 128), 1)
    g0, g1, g2, g3 = g_ref[0], g_ref[1], g_ref[2], g_ref[3]
    tiles = (
        jnp.where(lane < 96, g0, pltpu.roll(g1, 96, 1)),
        jnp.where(lane < 64, pltpu.roll(g1, 96, 1), pltpu.roll(g2, 64, 1)),
        jnp.where(lane < 32, pltpu.roll(g2, 64, 1), pltpu.roll(g3, 32, 1)),
    )
    first = ((lax.axis_index("x") * ZL + lax.axis_index("zl")) * (ZH * Y) + my_zh * Y + my_y) * C
    first = (first + mine) * ROWS
    base = pl.multiple_of(first // 16 * 16, 16)
    win_ref[:32, :] = w_ref[pl.ds(base, 32), :].astype(F32)
    wanted = first + lax.broadcasted_iota(jnp.int32, (8, 128), 0)
    column = lax.broadcasted_iota(jnp.int32, (8, 128), 1)
    found = jnp.zeros((8, 128), F32)
    centre = jnp.zeros((TOK, 128), F32)
    inv = inv_ref[...]
    cot = cot_ref[...]
    for at in range(0, D, CHUNK):
        grad = lax.dot_general(cot, w_ref[at : at + CHUNK, :], (((1,), (1,)), ((), ())), preferred_element_type=F32)
        for tile in range(CHUNK // 128):
            here = at + tile * 128
            number = here // 128
            gain = tiles[number % 3][number // 3 : number // 3 + 1, :]
            found += jnp.where(column + here == wanted, gain, 0.0)
            scaled = grad[:, tile * 128 : tile * 128 + 128] * gain
            sg_ref[:, here : here + 128] = scaled
            centre += scaled * (x_ref[:, here : here + 128].astype(F32) * inv)
    total = total_ref[...]
    weight_ref[...] = (total * jnp.sum(found, axis=1, keepdims=True))[:ROWS]
    gain_ref[...] = jnp.sum((total * win_ref[pl.ds(first - base, 8), :]).T, axis=0)[:ROWS]
    mean = jnp.broadcast_to(jnp.sum(centre, axis=1, keepdims=True) * (1.0 / D), (TOK, 128))
    for here in range(0, D, 128):
        normal = x_ref[:, here : here + 128].astype(F32) * inv
        grad_ref[:, here : here + 128] = (inv * (sg_ref[:, here : here + 128] - normal * mean)).astype(BF16)

def last_sum(parts_ref, total_ref):
    total = parts_ref[0]
    for place in range(1, LINE):
        total += parts_ref[place]
    total_ref[...] = total * (1.0 / DEVICES)

def call(body, outs, scratch=(), flops=0, moved=0, limit=40, **more):
    return pl.pallas_call(
        body,
        **more,
        out_shape=[jax.ShapeDtypeStruct(*o) for o in outs],
        scratch_shapes=list(scratch),
        compiler_params=pltpu.CompilerParams(vmem_limit_bytes=limit * MIB),
        cost_estimate=pl.CostEstimate(flops=flops, bytes_accessed=moved, transcendentals=0),
    )

def swap_cores(a):
    return lax.ppermute(a, "core", [(0, 1), (1, 0)])

def exchange(a, axis):
    return lax.all_to_all(a, axis, split_axis=0, concat_axis=0, tiled=True)

def shift(a, axis, n, by):
    return lax.ppermute(a, axis, [(i, (i + by) % n) for i in range(n)])

def on_device(layer_input, norm_gain, kv_weight, kv_cotangent):
    hbm = pl.BlockSpec(memory_space=pltpu.HBM)
    (slabs,) = call(
        make_slabs,
        [((Y, SLAB, H), BF16)],
        [pltpu.VMEM((SLAB, H), BF16), pltpu.VMEM((1, SHARD), BF16), pltpu.SemaphoreType.DMA((Y + 2,))],
        flops=int(2e10),
        limit=60,
        in_specs=[hbm, hbm],
        out_specs=[hbm],
    )(kv_weight, norm_gain.reshape(1, SHARD))
    column = exchange(slabs, "y")
    _, rows, cotangent = lax.optimization_barrier((slabs, layer_input, kv_cotangent))
    far, far_cot = swap_cores(rows), swap_cores(cotangent)
    turns = [shift(column, "zh", ZH, turn) for turn in range(1, ZH)]
    near, inv = call(
        near_terms,
        [((HALF, H), F32), ((TOK, 128), F32)],
        [pltpu.VMEM((D, H), F32)],
        flops=int(3e10),
        moved=2 * TOK * D + 2 * D * H,
    )(layer_input, kv_cotangent)
    (half,) = call(
        far_terms,
        [((PLANE * PADDED, H), F32)],
        [pltpu.VMEM((D, H), F32)],
        flops=4 * TOK * D * H,
        moved=2 * TOK * D + 4 * D * H,
    )(far, far_cot, kv_cotangent, near)
    parts = exchange(half.astype(F16).reshape(PLANE, PADDED, H), ("x", "y")).astype(F32)
    (sums,) = call(plane_sum, [((LINE, 8, H), F32)], [pltpu.VMEM((8 * LINE, H), F32)], flops=PLANE * PART * H, moved=4 * HALF * H)(parts)
    last = exchange(sums, ("zl", "zh"))
    turns, _ = lax.optimization_barrier((turns, sums))
    own = jnp.stack([column] + turns)
    other = swap_cores(own)

    (total,) = call(last_sum, [((8, H), F32)], flops=int(2e10), moved=LINE * 4096)(last)
    return call(
        outputs,
        [((TOK, D), BF16), ((ROWS, H), F32), ((ROWS,), F32)],
        [
            pltpu.VMEM((D + 32, H), BF16),
            pltpu.VMEM((4, 16, 128), F32),
            pltpu.VMEM((TOK, D), F32),
            pltpu.VMEM((32 + 8, H), F32),
        ],
        flops=2 * TOK * D * H,
        moved=4 * TOK * D,
    )(layer_input, kv_cotangent, inv, own, other, total)

def solution(mesh):
    axes = ("x", "zl", "zh", "y", "core")
    fine = Mesh(mesh.devices.reshape(X, ZL, ZH, Y, C), axes)
    intra = ("zh", "y", "core")
    return jax.shard_map(
        on_device,
        mesh=fine,
        in_specs=(P(axes, None), P(intra), P(intra, None), P(axes, None)),
        out_specs=(P(axes, None), P(axes, None), P(axes)),
        check_vma=False,
    )
```

```python
import jax
import jax.numpy as jnp
from jax import lax
from jax.experimental import pallas as pl
from jax.experimental.pallas import tpu as pltpu
from jax.sharding import Mesh, PartitionSpec as P

EPS = 1e-05
X, ZL, ZH, Y, C = 4, 4, 3, 8, 2
PLANE, LINE = X * Y, ZL * ZH
DEVICES = PLANE * LINE * C
TOK, D, H = 128, 4608, 128
ROWS = D // DEVICES
SHARD = D // (ZH * Y * C)
SLAB = SHARD + 16
HALF = D // C
PART = HALF // PLANE
PADDED = PART + 8
SIDE = LINE * Y
CHUNK = 512
BF16, F16, F32 = jnp.bfloat16, jnp.float16, jnp.float32
VMEM = pl.BlockSpec(memory_space=pltpu.VMEM)
MIB = 1024 * 1024

def make_slabs(w_ref, gain_ref, slabs_ref, slab, gain_row, sem):
    fetches = [
        pltpu.make_async_copy(gain_ref, gain_row, sem.at[Y]),
        pltpu.make_async_copy(w_ref, slab.at[:SHARD, :], sem.at[Y + 1]),
    ]
    for copy in fetches:
        copy.start()
    slab[SHARD:, :] = jnp.zeros((16, H), BF16)
    fetches[0].wait()
    slab[SHARD:, :SHARD] = jnp.broadcast_to(gain_row[...].astype(F32), (16, SHARD)).astype(BF16)
    fetches[1].wait()
    copies = [pltpu.make_async_copy(slab, slabs_ref.at[y], sem.at[y]) for y in range(Y)]
    for copy in copies:
        copy.start()
    for copy in copies:
        copy.wait()


def inverse(ref):
    square = jnp.zeros((TOK, 128), F32)
    for at in range(0, D, 128):
        wide = ref[:, at : at + 128].astype(F32)
        square += wide * wide
    return lax.rsqrt(jnp.sum(square, axis=1, keepdims=True) * (1.0 / D) + EPS)

def row_scales(x_ref, inv_ref):
    inv_ref[...] = jnp.broadcast_to(inverse(x_ref), (TOK, 128))


def row_terms(x_ref, far_ref, cot_ref, far_cot_ref, inv_ref, half_ref, all_ref):
    near, far = cot_ref[...].astype(F32), far_cot_ref[...].astype(F32)
    largest = jnp.max(jnp.maximum(jnp.abs(near), jnp.abs(far)), axis=(0, 1), keepdims=True)
    power = jnp.ceil(jnp.log2(jnp.maximum(largest, 1e-30)))
    scale = jnp.exp2(-power)
    scaled = jnp.concatenate([near * (inv_ref[...] * scale), far * (inverse(far_ref) * scale)], axis=0)
    high = scaled.astype(BF16)
    low = (scaled - high.astype(F32)).astype(BF16)
    parts = jnp.concatenate([high, low], axis=1)
    for at in range(0, D, CHUNK):
        turned = jnp.concatenate([x_ref[:, at : at + CHUNK].T, far_ref[:, at : at + CHUNK].T], axis=1)
        pair = jnp.dot(turned, parts, preferred_element_type=F32)
        all_ref[at : at + CHUNK, :] = pair[:, :H] + pair[:, H:]
    mine = lax.axis_index("core")
    for x in range(X):
        for row in range(ROWS):
            for place in range(LINE):
                start = x * (D // X) + place * SHARD + row + mine * ROWS
                to = pl.ds(x * Y * PADDED + row * LINE + place, Y, stride=PADDED)
                half_ref[to, :] = all_ref[pl.ds(start, Y, stride=C * ROWS), :]
    for chip in range(PLANE):
        half_ref[chip * PADDED + PART : (chip + 1) * PADDED, :] = jnp.broadcast_to(power, (8, H))


def plane_sum(parts_ref, out_ref, sum_ref):
    total = jnp.zeros((PART, H), F32)
    for chip in range(PLANE):
        total += parts_ref[chip, :PART] * jnp.exp2(parts_ref[chip, PART : PART + 1, :])
    sum_ref[:PART, :] = total
    sum_ref[PART:, :] = jnp.zeros((8 * LINE - PART, H), F32)
    for place in range(LINE):
        out_ref[place] = sum_ref[pl.ds(place, 8, stride=LINE), :]

def outputs(x_ref, cot_ref, inv_ref, own_ref, other_ref, total_ref, grad_ref, weight_ref, gain_ref, w_ref, g_ref, sg_ref, win_ref):
    mine, my_y, my_zh = lax.axis_index("core"), lax.axis_index("y"), lax.axis_index("zh")
    for turn in range(ZH):
        from_zh = lax.rem(my_zh + ZH - turn, ZH)
        for y in range(Y):
            for ref, core in ((own_ref, mine), (other_ref, 1 - mine)):
                shard = 2 * (from_zh * Y + y) + core
                w_ref[pl.ds(pl.multiple_of(shard * SHARD, SHARD), SHARD), :] = ref[turn, y, :SHARD, :]
                g_ref[lax.rem(shard, 4), pl.ds(shard // 4, 1), :] = ref[turn, y, SHARD:, :].astype(F32)[:1]
    w_ref[D:, :] = jnp.zeros((32, H), BF16)
    lane = lax.broadcasted_iota(jnp.int32, (16, 128), 1)
    g0, g1, g2, g3 = g_ref[0], g_ref[1], g_ref[2], g_ref[3]
    tiles = (
        jnp.where(lane < 96, g0, pltpu.roll(g1, 96, 1)),
        jnp.where(lane < 64, pltpu.roll(g1, 96, 1), pltpu.roll(g2, 64, 1)),
        jnp.where(lane < 32, pltpu.roll(g2, 64, 1), pltpu.roll(g3, 32, 1)),
    )
    first = ((lax.axis_index("x") * ZL + lax.axis_index("zl")) * (ZH * Y) + my_zh * Y + my_y) * C
    first = (first + mine) * ROWS
    base = pl.multiple_of(first // 16 * 16, 16)
    win_ref[:32, :] = w_ref[pl.ds(base, 32), :].astype(F32)
    wanted = first + lax.broadcasted_iota(jnp.int32, (8, 128), 0)
    column = lax.broadcasted_iota(jnp.int32, (8, 128), 1)
    found = jnp.zeros((8, 128), F32)
    centre = jnp.zeros((TOK, 128), F32)
    inv = inv_ref[...]
    cot = cot_ref[...]
    for at in range(0, D, CHUNK):
        grad = lax.dot_general(cot, w_ref[at : at + CHUNK, :], (((1,), (1,)), ((), ())), preferred_element_type=F32)
        for tile in range(CHUNK // 128):
            here = at + tile * 128
            number = here // 128
            gain = tiles[number % 3][number // 3 : number // 3 + 1, :]
            found += jnp.where(column + here == wanted, gain, 0.0)
            scaled = grad[:, tile * 128 : tile * 128 + 128] * gain
            sg_ref[:, here : here + 128] = scaled
            centre += scaled * x_ref[:, here : here + 128].astype(F32)
    total = total_ref[...]
    weight_ref[...] = (total * jnp.sum(found, axis=1, keepdims=True))[:ROWS]
    gain_ref[...] = jnp.sum((total * win_ref[pl.ds(first - base, 8), :]).T, axis=0)[:ROWS]
    pull = inv * inv * inv * (jnp.sum(centre, axis=1, keepdims=True) * (1.0 / D))
    for here in range(0, D, 128):
        wide = x_ref[:, here : here + 128].astype(F32)
        grad_ref[:, here : here + 128] = (inv * sg_ref[:, here : here + 128] - wide * pull).astype(BF16)


def last_sum(parts_ref, total_ref):
    total = parts_ref[0]
    for place in range(1, LINE):
        total += parts_ref[place]
    total_ref[...] = total * (1.0 / DEVICES)

def call(body, outs, scratch=(), flops=0, moved=0, limit=40, **more):
    return pl.pallas_call(
        body,
        **more,
        out_shape=[jax.ShapeDtypeStruct(*o) for o in outs],
        scratch_shapes=list(scratch),
        compiler_params=pltpu.CompilerParams(vmem_limit_bytes=limit * MIB),
        cost_estimate=pl.CostEstimate(flops=flops, bytes_accessed=moved, transcendentals=0),
    )

def swap_cores(a):
    return lax.ppermute(a, "core", [(0, 1), (1, 0)])

def exchange(a, axis):
    return lax.all_to_all(a, axis, split_axis=0, concat_axis=0, tiled=True)

def shift(a, axis, n, by):
    return lax.ppermute(a, axis, [(i, (i + by) % n) for i in range(n)])

def on_device(layer_input, norm_gain, kv_weight, kv_cotangent):
    hbm = pl.BlockSpec(memory_space=pltpu.HBM)
    (slabs,) = call(
        make_slabs,
        [((Y, SLAB, H), BF16)],
        [pltpu.VMEM((SLAB, H), BF16), pltpu.VMEM((1, SHARD), BF16), pltpu.SemaphoreType.DMA((Y + 2,))],
        flops=int(2e10),
        limit=60,
        in_specs=[hbm, hbm],
        out_specs=[hbm],
    )(kv_weight, norm_gain.reshape(1, SHARD))
    column = exchange(slabs, "y")
    _, rows, cotangent = lax.optimization_barrier((slabs, layer_input, kv_cotangent))
    far, far_cot = swap_cores(rows), swap_cores(cotangent)
    turns = [shift(column, "zh", ZH, turn) for turn in range(1, ZH)]
    (inv,) = call(row_scales, [((TOK, 128), F32)], flops=int(3e10))(layer_input)
    (half,) = call(row_terms, [((PLANE * PADDED, H), F32)], [pltpu.VMEM((D, H), F32)])(layer_input, far, kv_cotangent, far_cot, inv)
    parts = exchange(half.astype(F16).reshape(PLANE, PADDED, H), ("x", "y")).astype(F32)
    (sums,) = call(plane_sum, [((LINE, 8, H), F32)], [pltpu.VMEM((8 * LINE, H), F32)], flops=PLANE * PART * H, moved=4 * HALF * H)(parts)
    last = exchange(sums, ("zl", "zh"))
    turns, _ = lax.optimization_barrier((turns, sums))
    own = jnp.stack([column] + turns)
    other = swap_cores(own)

    (total,) = call(last_sum, [((8, H), F32)], flops=int(2e10), moved=LINE * 4096)(last)
    return call(
        outputs,
        [((TOK, D), BF16), ((ROWS, H), F32), ((ROWS,), F32)],
        [
            pltpu.VMEM((D + 32, H), BF16),
            pltpu.VMEM((4, 16, 128), F32),
            pltpu.VMEM((TOK, D), F32),
            pltpu.VMEM((32 + 8, H), F32),
        ],
        flops=2 * TOK * D * H,
        moved=4 * TOK * D,
    )(layer_input, kv_cotangent, inv, own, other, total)

def solution(mesh):
    axes = ("x", "zl", "zh", "y", "core")
    fine = Mesh(mesh.devices.reshape(X, ZL, ZH, Y, C), axes)
    intra = ("zh", "y", "core")
    return jax.shard_map(
        on_device,
        mesh=fine,
        in_specs=(P(axes, None), P(intra), P(intra, None), P(axes, None)),
        out_specs=(P(axes, None), P(axes, None), P(axes)),
        check_vma=False,
    )
```
